32 devices in a mesh: shot: 2 (over y), sx: 8 (over z, x), sy: 2 (over core).
Axes of the slice: x: 2, y: 2, z: 4, core: 2. Of those that a mesh axis runs over, the one named last changes fastest.
Arguments:
- pressure: float32 [256, 32, 128], P(('shot', 'sx'), 'sy'), parts along dimension 0, may hold values from -6 to 6
- velocity: float32 [3, 256, 32, 128], P(None, ('shot', 'sx'), 'sy'), parts along dimension 1, may hold values from -6 to 6
- courant: float32 [128, 32, 128], P('sx', 'sy'), may hold values from 0.15 to 0.42
- observed: float32 [4096, 2000], P(('shot', 'sx', 'sy')), parts along dimension 0, may hold values from -6 to 6
- rec_owner: int32 [4096, 1], P(('shot', 'sx', 'sy')), parts along dimension 0, may hold values from 0 to 15; in each aligned block of 128 rows (0 to 127, 128 to 255, ...) at most 16 rows name the same one
- rec_cell: int32 [4096], P(('shot', 'sx', 'sy')), parts along dimension 0, may hold values from 0 to 32767
- src_pos: int32 [2], P('shot'), parts along dimension 0, may hold values from 0 to 524287
- wavelet: float32 [20], replicated, may hold values from -4 to 4
Outputs:
- pressure_out: float32 [256, 32, 128], P(('shot', 'sx'), 'sy'), parts along dimension 0
- velocity_out: float32 [3, 256, 32, 128], P(None, ('shot', 'sx'), 'sy'), parts along dimension 1
- trace_xcorr: float32 [3962], P('shot'), parts along dimension 0
The draws below stay inside these ranges and needn't reach their ends.
There are 2 independent parts, one for each index of `shot`. The reference program is written for one: setup_inputs(seed, part) draws one part's arguments, and reference() takes and returns one part's arrays. A program takes and returns all parts, laid end to end along the dimension named above; an argument that names none is the same for every part. Nothing has to cross between parts.
Inputs may be any that keep to these rules, and one draw needn't show every extreme that they name: `rec_owner`: in each device's block of 128 receivers at most 16 have the same owner; in some blocks one owner has exactly 16.
All inputs are finite; a program needn't handle non-finite values.
Results may differ from the reference program's by a relative error of at most 0.00022.
Values sent between devices are 32-bit elements; how exact they have to be, the bound alone decides.
A program may use at most 64 MiB of HBM per device.

```python
import math
import jax
import jax.numpy as jnp
import numpy as np
from jax import lax

CX = 16
CY = 16
CZ = 128
STEPS = 20
NT = 2000
R_DEV = 128
SUBDOMAINS = 16
CAP = 16
RECV = 2048
NX = 128
NY = 32
N_SY = 2


def plant(array, stream_key, smallest, high):
    spot = [jax.random.randint(jax.random.fold_in(stream_key, axis), (), 0, length) for axis, length in enumerate(array.shape)]
    widest = array.shape.index(max(array.shape))
    next_to = spot[:widest] + [(spot[widest] + 1) % array.shape[widest]] + spot[widest + 1:]
    return array.at[tuple(spot)].set(smallest).at[tuple(next_to)].set(high)


def levels(rng, shape, pieces, smallest, high):
    def one(position, shards_of):
        steps = jax.random.uniform(jax.random.fold_in(jax.random.fold_in(rng, 6), position), (shards_of,), jnp.float32, smallest / len(pieces), high / len(pieces))
        return jnp.repeat(jnp.exp(steps), shape[position] // shards_of).reshape((-1,) + (1,) * (len(shape) - position - 1))

    gain = one(*pieces[0])
    for cut in pieces[1:]:
        gain = gain * one(*cut)
    return gain


def routed_block(rng, own, number, rows, number_of, top, reach, lean):
    ranking = jax.random.permutation(rng, number_of)
    crowded, common = portions_of(number_of, rows * top, reach, lean, True), portions_of(number_of, rows * top, reach, lean, False)
    places = jnp.arange(number_of)

    def named(sizes, turn):
        used = int((sizes > 0).sum())
        fixed = max(1, used // 4)
        moved = fixed + (places - fixed + turn * (used - fixed)) % max(1, number_of - fixed)
        return jnp.zeros((number_of,), jnp.int32).at[ranking[jnp.where(places < fixed, places, moved)]].set(jnp.asarray(sizes, jnp.int32))

    sizes = jnp.where(number % 4 == 0, named(crowded, number // 4), named(common, number - number // 4 - 1))
    mixed = jax.random.permutation(jax.random.fold_in(own, 3), number_of)
    giver, receiver = mixed[0:number_of // 2 * 2:2], mixed[1:number_of // 2 * 2:2]
    margin = jnp.minimum(sizes[giver] - 1, reach - sizes[receiver]) // 2
    margin = jnp.where((giver == ranking[0]) | (receiver == ranking[0]) | (sizes[receiver] == 0), 0, jnp.maximum(margin, 0))
    moved = jax.random.randint(jax.random.fold_in(own, 4), (number_of // 2,), 0, 1 << 20) % (margin + 1)
    sizes = sizes.at[giver].add(-moved).at[receiver].add(moved)
    members = jnp.searchsorted(jnp.cumsum(sizes), jnp.arange(rows * top), side="right").astype(jnp.int32)
    grid = members.reshape(top, rows).T
    grid = grid[jax.random.permutation(jax.random.fold_in(own, 1), rows)]
    turn = jax.random.randint(jax.random.fold_in(own, 2), (rows, 1), 0, top)
    return jnp.take_along_axis(grid, (jnp.arange(top)[None, :] + turn) % top, axis=1)


def portions_of(number_of, total, bound, lean, full):
    loads = [(1 << 20) // math.isqrt(standing ** lean) + 1 for standing in range(1, number_of + 1)]
    largest = bound if full else min(bound, max(-(-total // number_of), total * loads[0] // sum(loads)))
    least = 1 if total - largest >= number_of - 1 else 0
    holding, rest = [largest] + [least] * (number_of - 1), total - largest - least * (number_of - 1)
    while rest > 0:
        movable = [i for i in range(1, number_of) if holding[i] < largest] or [i for i in range(1, number_of) if holding[i] < bound]
        mass, remaining = sum([loads[i] for i in movable]), rest
        for i in movable:
            more = min(bound - holding[i], max(1, remaining * loads[i] // mass), rest)
            holding[i] = holding[i] + more
            rest = rest - more
    return np.array(holding)


def scatter_about(stream_key, dims, spread, limit, pieces=(), held_as=jnp.bfloat16):
    loudness = levels(stream_key, dims, pieces, -0.22, 0.18) if pieces else 1.0
    array = jax.random.normal(stream_key, dims, jnp.float32) * spread * loudness
    return jnp.minimum(jnp.maximum(array, -limit), limit).astype(held_as)


def setup_inputs(seed: int = 0, part: int = 0) -> dict:
    splits = jax.random.split(jax.random.key(seed), 9)
    own_keys = jax.random.split(jax.random.fold_in(splits[8], part), 9)
    pressure = scatter_about(own_keys[0], (NX, NY, CZ), 1.0, 6.0, ((0, 8), (1, 2)), jnp.float32)
    velocity = scatter_about(own_keys[1], (3, NX, NY, CZ), 1.0, 6.0, ((1, 8), (2, 2)), jnp.float32)
    courant = jnp.clip(0.15 + 0.26999998 * jax.random.uniform(splits[2], (NX, NY, CZ), jnp.float32) ** levels(splits[2], (NX, NY, CZ), ((0, 8), (1, 2)), -0.2, 0.2), 0.15, 0.42)
    observed = scatter_about(own_keys[3], (RECV, NT), 1.0, 6.0, ((0, 16),), jnp.float32)
    rec_owner_keys = jax.random.split(jax.random.fold_in(own_keys[4], 1), RECV // R_DEV)
    rec_owner_turns = jax.random.permutation(jax.random.fold_in(own_keys[4], 3), RECV // R_DEV)
    rec_owner = jax.vmap(lambda own, number: routed_block(jax.random.fold_in(own_keys[4], 2), own, number, R_DEV, SUBDOMAINS, 1, CAP, 2))(rec_owner_keys, rec_owner_turns).reshape((RECV, 1))
    rec_cell = plant(jax.random.randint(own_keys[5], (RECV,), 0, CX * CY * CZ), jax.random.fold_in(own_keys[5], 1), 0, (CX * CY * CZ) - 1).astype(jnp.int32)
    src_pos = jax.random.randint(own_keys[6], (1,), 0, NX * NY * CZ).astype(jnp.int32)
    wavelet = scatter_about(splits[7], (STEPS,), 1.0, 4.0, (), jnp.float32)
    return dict(pressure=pressure, velocity=velocity, courant=courant, observed=observed, rec_owner=rec_owner, rec_cell=rec_cell, src_pos=src_pos, wavelet=wavelet)


c_one = 9.0 / 8.0
c_two = -1.0 / 24.0

def ahead(padded, axis, count):

    def part(k):
        return lax.slice_in_dim(padded, 2 + k, 2 + k + count, axis=axis)
    return c_one * (part(1) - part(0)) + c_two * (part(2) - part(-1))

def behind(padded, axis, count):

    def part(k):
        return lax.slice_in_dim(padded, 2 + k, 2 + k + count, axis=axis)
    return c_one * (part(0) - part(-1)) + c_two * (part(1) - part(-2))

def padded_on(field, axis):
    widths = [(0, 0)] * field.ndim
    widths[axis] = (2, 2)
    return jnp.pad(field, widths)

def reference(pressure, velocity, courant, observed, rec_owner, rec_cell, src_pos, wavelet):
    nx, ny, nz = pressure.shape
    total = nx * ny * nz
    source_mask = (jnp.arange(total, dtype=jnp.int32) == src_pos[0]).astype(jnp.float32).reshape(nx, ny, nz)
    owner = rec_owner[:, 0]
    owner_x = owner // N_SY
    owner_y = owner % N_SY
    local_x = rec_cell // (CY * CZ)
    local_y = rec_cell // CZ % CY
    local_z = rec_cell % CZ
    global_cell = ((owner_x * CX + local_x) * ny + (owner_y * CY + local_y)) * nz + local_z
    global_cell = global_cell.astype(jnp.int32)
    press = pressure
    vel_x, vel_y, vel_z = (velocity[0], velocity[1], velocity[2])
    records = []
    for step in range(STEPS):
        vel_x = vel_x - courant * ahead(padded_on(press, 0), 0, nx)
        vel_y = vel_y - courant * ahead(padded_on(press, 1), 1, ny)
        vel_z = vel_z - courant * ahead(padded_on(press, 2), 2, nz)
        diverge = behind(padded_on(vel_x, 0), 0, nx) + behind(padded_on(vel_y, 1), 1, ny)
        diverge = diverge + behind(padded_on(vel_z, 2), 2, nz)
        press = press - courant * diverge
        press = press + wavelet[step] * source_mask
        records.append(press.reshape(-1)[global_cell])
    nlag = NT - STEPS + 1
    summed = jnp.zeros((nlag,), jnp.float32)
    for step in range(STEPS):
        window = lax.slice_in_dim(observed, step, step + nlag, axis=1)
        summed = summed + jnp.dot(records[step], window, precision=lax.Precision.HIGHEST)
    scale = 1.0 / math.sqrt(RECV * STEPS)
    return (press, jnp.stack([vel_x, vel_y, vel_z]), summed * scale)
```

```python
import functools
import math

import jax
import jax.numpy as jnp
from jax import lax
from jax.experimental import pallas as pl
from jax.experimental.pallas import tpu as pltpu
from jax.sharding import PartitionSpec as P

c_one = 9.0 / 8.0
c_two = -1.0 / 24.0
HALO = 3
SIDE = 8


def pieces(value, count):
    parts = []
    for _ in range(count):
        part = value.astype(jnp.bfloat16)
        parts.append(part)
        value = value - part.astype(jnp.float32)
    return parts


def slope(a, b, c, d):
    return c_one * (a - b) + c_two * (c - d)


def shifted(f, k, axis):
    count = f.shape[axis]
    return pltpu.roll(f, (-k) % count, axis)


def shifted_z(f, k):
    count = f.shape[-1]
    place = lax.broadcasted_iota(jnp.int32, f.shape, f.ndim - 1)
    keep = place < count - k if k > 0 else place >= -k
    return jnp.where(keep, shifted(f, k, f.ndim - 1), 0.0)


def kernel(
    count_x,
    count_y,
    cap,
    press_ref,
    vel_ref,
    cour_ref,
    obs_ref,
    owner_ref,
    cell_ref,
    src_ref,
    wave_ref,
    press_out,
    vel_out,
    xc_out,
    field,
    speed,
    edge_x,
    edge_y,
    base,
    mark,
    now,
    codes_out,
    codes_in,
    rows_hot,
    lane_hot,
    records,
    returned,
    table,
    sums,
    halo_send,
    halo_recv,
    once_send,
    once_recv,
    swap_send,
    swap_recv,
):
    cx, cy, cz = press_ref.shape
    r_dev, nt = obs_ref.shape
    steps = wave_ref.shape[0]
    nlag = nt - steps + 1
    subs = count_x * count_y
    slots = subs * cap
    ix = lax.axis_index("sx")
    iy = lax.axis_index("sy")
    me = ix * count_y + iy
    inner = pl.ds(SIDE, cy)

    def place_of(peer):
        return {"sx": peer // count_y, "sy": peer % count_y}

    def peer_at(k):
        return lax.rem(me + k, subs)

    field[...] = jnp.zeros_like(field)
    speed[...] = jnp.zeros_like(speed)
    edge_x[...] = jnp.zeros_like(edge_x)
    edge_y[...] = jnp.zeros_like(edge_y)

    barrier = pltpu.get_barrier_semaphore()

    def greet(k, carry):
        pl.semaphore_signal(
            barrier, inc=1, device_id=place_of(peer_at(k)), device_id_type=pl.DeviceIdType.MESH
        )
        return carry

    lax.fori_loop(1, subs, greet, 0)

    low = {"sx": ix - 1}
    high = {"sx": ix + 1}
    beside = {"sy": 1 - iy}
    has_low = ix > 0
    has_high = ix < count_x - 1

    def remote(src, dst, send, recv, device):
        return pltpu.make_async_remote_copy(
            src_ref=src,
            dst_ref=dst,
            send_sem=send,
            recv_sem=recv,
            device_id=device,
            device_id_type=pl.DeviceIdType.MESH,
        )

    y_from = pl.multiple_of(SIDE * (1 - iy), SIDE)
    y_to = pl.multiple_of((SIDE + cy) * iy, SIDE)
    y_rows = pl.ds(y_from + SIDE, SIDE)
    y_land = pl.ds(y_to, SIDE)
    y_own = pl.ds(y_from, SIDE)
    mid = pl.ds(HALO, cx)
    top = pl.ds(HALO + cx, HALO)
    bottom = pl.ds(0, HALO)

    def to_low(b):
        return remote(
            field.at[b, pl.ds(HALO, HALO), inner],
            field.at[b, top, inner],
            halo_send.at[0, b],
            halo_recv.at[0, b],
            low,
        )

    def to_high(b):
        return remote(
            field.at[b, pl.ds(cx, HALO), inner],
            field.at[b, bottom, inner],
            halo_send.at[1, b],
            halo_recv.at[1, b],
            high,
        )

    def to_side(b):
        return remote(
            field.at[b, mid, y_rows],
            field.at[b, mid, y_land],
            halo_send.at[2, b],
            halo_recv.at[2, b],
            beside,
        )

    def once_low():
        part = pl.ds(0, HALO)
        return [
            remote(cour_ref.at[part], speed.at[top, inner], once_send.at[0], once_recv.at[0], low),
            remote(vel_ref.at[0, part], edge_x.at[top], once_send.at[1], once_recv.at[1], low),
        ]

    def once_high():
        part = pl.ds(cx - HALO, HALO)
        return [
            remote(cour_ref.at[part], speed.at[bottom, inner], once_send.at[2], once_recv.at[2], high),
            remote(vel_ref.at[0, part], edge_x.at[bottom], once_send.at[3], once_recv.at[3], high),
        ]

    def once_side():
        return [
            remote(
                cour_ref.at[:, y_own], speed.at[mid, y_land], once_send.at[4], once_recv.at[4], beside
            ),
            remote(
                vel_ref.at[1, :, y_own], edge_y.at[:, y_land], once_send.at[5], once_recv.at[5], beside
            ),
        ]

    lane = lax.broadcasted_iota(jnp.int32, (r_dev, r_dev), 1)
    row = lax.broadcasted_iota(jnp.int32, (r_dev, r_dev), 0)
    down = jnp.broadcast_to(owner_ref[...], (r_dev, r_dev)).astype(jnp.float32)
    across = jnp.sum(jnp.where(lane == row, down, 0.0), axis=0, keepdims=True)
    earlier = jnp.where((down == across) & (row < lane), 1.0, 0.0)
    rank = jnp.sum(earlier, axis=0, keepdims=True)
    spot = (across * float(cap) + rank).astype(jnp.int32)
    slot_id = lax.broadcasted_iota(jnp.int32, (slots, r_dev), 0)
    chosen = slot_id == spot
    code = (cell_ref[...] + 1).astype(jnp.float32)
    packed = jnp.sum(jnp.where(chosen, code, 0.0), axis=1, keepdims=True)
    codes_out[...] = jnp.broadcast_to(packed, codes_out.shape)

    field[0, HALO : HALO + cx, SIDE : SIDE + cy, :] = press_ref[...]
    speed[HALO : HALO + cx, SIDE : SIDE + cy, :] = cour_ref[...]
    edge_x[HALO : HALO + cx] = vel_ref[0]
    edge_y[:, SIDE : SIDE + cy, :] = vel_ref[1]
    now[...] = press_ref[...]
    records[...] = jnp.zeros_like(records)

    pl.semaphore_wait(barrier, subs - 1)

    @pl.when(has_low)
    def _():
        to_low(0).start()
        for copy in once_low():
            copy.start()

    @pl.when(has_high)
    def _():
        to_high(0).start()
        for copy in once_high():
            copy.start()

    to_side(0).start()
    for copy in once_side():
        copy.start()

    def swap(stage, source, landing, k):
        peer = peer_at(k)
        return remote(
            source.at[pl.ds(pl.multiple_of(peer * cap, 8), cap)],
            landing.at[pl.ds(pl.multiple_of(me * cap, 8), cap)],
            swap_send.at[stage, k],
            swap_recv.at[stage, k],
            place_of(peer),
        )

    def share(k):
        return remote(
            sums.at[me], sums.at[me], swap_send.at[2, k], swap_recv.at[2, k], place_of(peer_at(k))
        )

    def each(action):
        def one(k, carry):
            action(k)
            return carry

        lax.fori_loop(1, subs, one, 0)

    each(lambda k: swap(0, codes_out, codes_in, k).start())
    own = pl.ds(pl.multiple_of(me * cap, 8), cap)
    codes_in[own, :] = codes_out[own, :]

    shape = (cx, cy, cz)
    gx = lax.broadcasted_iota(jnp.int32, shape, 0) + ix * cx
    gy = lax.broadcasted_iota(jnp.int32, shape, 1) + iy * cy
    gz = lax.broadcasted_iota(jnp.int32, shape, 2)
    mark[...] = jnp.where((gx * (cy * count_y) + gy) * cz + gz == src_ref[0], 1.0, 0.0)

    @pl.when(has_low)
    def _():
        for copy in once_low():
            copy.wait_send()
        for copy in once_high():
            copy.wait_recv()

    @pl.when(has_high)
    def _():
        for copy in once_high():
            copy.wait_send()
        for copy in once_low():
            copy.wait_recv()

    for copy in once_side():
        copy.wait()

    fx = edge_x[1 : cx + 4]
    fy = edge_y[...]
    fz = vel_ref[2]
    spread = slope(fx[2 : 2 + cx], fx[1 : 1 + cx], fx[3 : 3 + cx], fx[0:cx])
    spread_y = slope(fy, shifted(fy, -1, 1), shifted(fy, 1, 1), shifted(fy, -2, 1))
    spread = spread + spread_y[:, SIDE : SIDE + cy]
    spread = spread + slope(fz, shifted_z(fz, -1), shifted_z(fz, 1), shifted_z(fz, -2))
    base[...] = cour_ref[...] * spread

    def grads(b, first, last):
        n = last - first
        fx = field[b, first : last + 2 * HALO, SIDE : SIDE + cy, :]
        m = n + 3
        grad_x = speed[first + 1 : last + 4, SIDE : SIDE + cy, :] * slope(
            fx[2 : 2 + m], fx[1 : 1 + m], fx[3 : 3 + m], fx[0:m]
        )
        fy = field[b, first + HALO : last + HALO]
        grad_y = speed[first + HALO : last + HALO] * slope(
            shifted(fy, 1, 1), fy, shifted(fy, 2, 1), shifted(fy, -1, 1)
        )
        fz = fy[:, SIDE : SIDE + cy]
        cour = cour_ref[first:last]
        grad_z = cour * slope(shifted_z(fz, 1), fz, shifted_z(fz, 2), shifted_z(fz, -1))
        return (grad_x, grad_y, grad_z, fz, cour)

    def update(b, first, last, amplitude):
        n = last - first
        grad_x, grad_y, grad_z, total, cour = grads(b, first, last)
        acc = slope(grad_x[2 : 2 + n], grad_x[1 : 1 + n], grad_x[3 : 3 + n], grad_x[0:n])
        acc_y = slope(
            grad_y, shifted(grad_y, -1, 1), shifted(grad_y, 1, 1), shifted(grad_y, -2, 1)
        )
        acc = acc + acc_y[:, SIDE : SIDE + cy]
        acc = acc + slope(
            grad_z, shifted_z(grad_z, -1), shifted_z(grad_z, 1), shifted_z(grad_z, -2)
        )
        fresh = now[first:last] + (cour * acc - base[first:last]) + amplitude * mark[first:last]
        now[first:last] = fresh
        field[1 - b, first + HALO : last + HALO, SIDE : SIDE + cy, :] = total + fresh

    def listen():
        each(lambda k: swap(0, codes_out, codes_in, k).wait())
        cell = codes_in[...].astype(jnp.int32) - 1
        bits = cz.bit_length() - 1
        cell_row = lax.shift_right_arithmetic(cell, jnp.full_like(cell, bits))
        cell_lane = cell & (cz - 1)
        lanes = lax.broadcasted_iota(jnp.int32, (slots, cz), 1)
        lane_hot[...] = jnp.where(cell_lane == lanes, 1.0, 0.0)
        for j in range(cx * cy // cz):
            rows_hot[:, j * cz : (j + 1) * cz] = jnp.where(
                cell_row == lanes + j * cz, 1.0, 0.0
            ).astype(jnp.bfloat16)

    def record(t):
        flat = now[...].reshape(cx * cy, cz)
        picked = jnp.zeros((slots, cz), jnp.float32)
        for part in pieces(flat, 3):
            picked = picked + jnp.dot(rows_hot[...], part, preferred_element_type=jnp.float32)
        value = jnp.sum(picked * lane_hot[...], axis=1, keepdims=True)
        lanes = lax.broadcasted_iota(jnp.int32, (slots, cz), 1)
        records[...] = jnp.where(lanes == t, value, records[...])

    listen()

    def advance(t, carry):
        b = lax.rem(t, 2)
        more = t < steps - 1

        @pl.when(has_low)
        def _():
            to_low(b).wait_send()
            to_high(b).wait_recv()

        @pl.when(has_high)
        def _():
            to_high(b).wait_send()
            to_low(b).wait_recv()

        to_side(b).wait()
        amplitude = wave_ref[t]
        update(b, 0, HALO, amplitude)

        @pl.when(has_low & more)
        def _():
            to_low(1 - b).start()

        update(b, cx - HALO, cx, amplitude)

        @pl.when(has_high & more)
        def _():
            to_high(1 - b).start()

        update(b, HALO, cx - HALO, amplitude)

        @pl.when(more)
        def _():
            to_side(1 - b).start()

        record(t)
        return carry

    lax.fori_loop(0, steps, advance, 0)

    each(lambda k: swap(1, records, returned, k).start())
    returned[own, :] = records[own, :]

    grad_x, grad_y, grad_z, _, _ = grads((steps - 1) % 2, 0, cx)
    vel_out[0] = vel_ref[0] - grad_x[2 : 2 + cx]
    vel_out[1] = vel_ref[1] - grad_y[:, SIDE : SIDE + cy]
    vel_out[2] = vel_ref[2] - grad_z
    press_out[...] = now[...]

    each(lambda k: swap(1, records, returned, k).wait())
    height = table.shape[0]
    by_step = jnp.transpose(returned[...])[0:height]
    hot = jnp.where(chosen, 1.0, 0.0).astype(jnp.bfloat16)
    syn = jnp.zeros((height, r_dev), jnp.float32)
    for part in pieces(by_step, 3):
        syn = syn + jnp.dot(part, hot, preferred_element_type=jnp.float32)
    table[...] = jnp.zeros_like(table)
    table[:, 0:nt] = jnp.dot(
        syn, obs_ref[...], precision=lax.Precision.HIGHEST, preferred_element_type=jnp.float32
    )
    lines = table[...]
    step_id = lax.broadcasted_iota(jnp.int32, lines.shape, 0)
    for bit in range((steps - 1).bit_length()):
        lines = jnp.where((step_id & (1 << bit)) != 0, shifted(lines, 1 << bit, 1), lines)
    scale = 1.0 / math.sqrt(subs * r_dev * steps)
    sums[me] = jnp.sum(lines, axis=0, keepdims=True) * scale
    each(lambda k: share(k).start())
    each(lambda k: share(k).wait())
    xc_out[...] = jnp.sum(sums[...], axis=0)


def body(pressure, velocity, courant, observed, rec_owner, rec_cell, src_pos, wavelet):
    cx, cy, cz = pressure.shape
    count_x = lax.axis_size("sx")
    count_y = lax.axis_size("sy")
    subs = count_x * count_y
    r_dev, nt = observed.shape
    steps = wavelet.shape[0]
    nlag = nt - steps + 1
    cap = -(-max(2, 2 * r_dev // subs) // 8) * 8
    slots = subs * cap
    wide = -(-nt // 128) * 128
    height = -(-steps // 8) * 8
    deep = cx + 2 * HALO
    tall = cy + 2 * SIDE
    f32 = jnp.float32
    vmem = pl.BlockSpec(memory_space=pltpu.VMEM)
    smem = pl.BlockSpec(memory_space=pltpu.SMEM)
    press, vel, xc = pl.pallas_call(
        functools.partial(kernel, count_x, count_y, cap),
        out_shape=(
            jax.ShapeDtypeStruct((cx, cy, cz), f32),
            jax.ShapeDtypeStruct((3, cx, cy, cz), f32),
            jax.ShapeDtypeStruct((1, wide), f32),
        ),
        in_specs=[vmem] * 6 + [smem] * 2,
        out_specs=(vmem,) * 3,
        scratch_shapes=[
            pltpu.VMEM((2, deep, tall, cz), f32),
            pltpu.VMEM((deep, tall, cz), f32),
            pltpu.VMEM((deep, cy, cz), f32),
            pltpu.VMEM((cx, tall, cz), f32),
            pltpu.VMEM((cx, cy, cz), f32),
            pltpu.VMEM((cx, cy, cz), f32),
            pltpu.VMEM((cx, cy, cz), f32),
            pltpu.VMEM((slots, cz), f32),
            pltpu.VMEM((slots, cz), f32),
            pltpu.VMEM((slots, cx * cy), jnp.bfloat16),
            pltpu.VMEM((slots, cz), f32),
            pltpu.VMEM((slots, cz), f32),
            pltpu.VMEM((slots, cz), f32),
            pltpu.VMEM((height, wide), f32),
            pltpu.VMEM((subs, 1, wide), f32),
            pltpu.SemaphoreType.DMA((3, 2)),
            pltpu.SemaphoreType.DMA((3, 2)),
            pltpu.SemaphoreType.DMA((6,)),
            pltpu.SemaphoreType.DMA((6,)),
            pltpu.SemaphoreType.DMA((3, subs)),
            pltpu.SemaphoreType.DMA((3, subs)),
        ],
        compiler_params=pltpu.CompilerParams(
            collective_id=0, has_side_effects=True, vmem_limit_bytes=40 * 2**20
        ),
    )(
        pressure,
        velocity,
        courant,
        observed,
        rec_owner,
        rec_cell.reshape(1, r_dev),
        src_pos,
        wavelet,
    )
    return (press, vel, xc[0, :nlag])


def solution(mesh):
    placed = (
        P(("shot", "sx"), "sy", None),
        P(None, ("shot", "sx"), "sy", None),
        P("sx", "sy", None),
        P(("shot", "sx", "sy"), None),
        P(("shot", "sx", "sy"), None),
        P(("shot", "sx", "sy")),
        P("shot"),
        P(),
    )
    return jax.shard_map(
        body,
        mesh=mesh,
        in_specs=placed,
        out_specs=(P(("shot", "sx"), "sy", None), P(None, ("shot", "sx"), "sy", None), P("shot")),
        check_vma=False,
    )
```

```python
import functools
import math

import jax
import jax.numpy as jnp
from jax import lax
from jax.experimental import pallas as pl
from jax.experimental.pallas import tpu as pltpu
from jax.sharding import PartitionSpec as P

c_one = 9.0 / 8.0
c_two = -1.0 / 24.0
HALO = 3
SIDE = 8


def pieces(value, count):
    parts = []
    for _ in range(count):
        part = value.astype(jnp.bfloat16)
        parts.append(part)
        value = value - part.astype(jnp.float32)
    return parts


def slope(a, b, c, d):
    return c_one * (a - b) + c_two * (c - d)


def shifted(f, k, axis):
    count = f.shape[axis]
    return pltpu.roll(f, (-k) % count, axis)


def shifted_z(f, k):
    count = f.shape[-1]
    place = lax.broadcasted_iota(jnp.int32, f.shape, f.ndim - 1)
    keep = place < count - k if k > 0 else place >= -k
    return jnp.where(keep, shifted(f, k, f.ndim - 1), 0.0)


def kernel(
    count_x,
    count_y,
    cap,
    press_ref,
    vel_ref,
    cour_ref,
    obs_far,
    owner_ref,
    cell_ref,
    src_ref,
    wave_ref,
    press_out,
    vel_out,
    xc_out,
    field,
    speed,
    edge_x,
    edge_y,
    base,
    mark,
    now,
    codes_out,
    codes_in,
    rows_hot,
    lane_hot,
    records,
    returned,
    table,
    sums,
    halo_send,
    halo_recv,
    once_send,
    once_recv,
    swap_send,
    swap_recv,
    obs_ref,
    obs_sem,
):
    cx, cy, cz = press_ref.shape
    r_dev, nt = obs_ref.shape
    steps = wave_ref.shape[0]
    nlag = nt - steps + 1
    subs = count_x * count_y
    slots = subs * cap
    ix = lax.axis_index("sx")
    iy = lax.axis_index("sy")
    me = ix * count_y + iy
    inner = pl.ds(SIDE, cy)

    def place_of(peer):
        return {"sx": peer // count_y, "sy": peer % count_y}

    def peer_at(k):
        return lax.rem(me + k, subs)

    fetch = pltpu.make_async_copy(obs_far, obs_ref, obs_sem.at[0])
    fetch.start()
    field[...] = jnp.zeros_like(field)
    speed[...] = jnp.zeros_like(speed)
    edge_x[...] = jnp.zeros_like(edge_x)
    edge_y[...] = jnp.zeros_like(edge_y)

    barrier = pltpu.get_barrier_semaphore()

    def greet(k, carry):
        pl.semaphore_signal(
            barrier, inc=1, device_id=place_of(peer_at(k)), device_id_type=pl.DeviceIdType.MESH
        )
        return carry

    lax.fori_loop(1, subs, greet, 0)

    low = {"sx": ix - 1}
    high = {"sx": ix + 1}
    beside = {"sy": 1 - iy}
    has_low = ix > 0
    has_high = ix < count_x - 1

    def remote(src, dst, send, recv, device):
        return pltpu.make_async_remote_copy(
            src_ref=src,
            dst_ref=dst,
            send_sem=send,
            recv_sem=recv,
            device_id=device,
            device_id_type=pl.DeviceIdType.MESH,
        )

    y_from = pl.multiple_of(SIDE * (1 - iy), SIDE)
    y_to = pl.multiple_of((SIDE + cy) * iy, SIDE)
    y_rows = pl.ds(y_from + SIDE, SIDE)
    y_land = pl.ds(y_to, SIDE)
    y_own = pl.ds(y_from, SIDE)
    mid = pl.ds(HALO, cx)
    top = pl.ds(HALO + cx, HALO)
    bottom = pl.ds(0, HALO)

    def to_low(b):
        return remote(
            field.at[b, pl.ds(HALO, HALO), inner],
            field.at[b, top, inner],
            halo_send.at[0, b],
            halo_recv.at[0, b],
            low,
        )

    def to_high(b):
        return remote(
            field.at[b, pl.ds(cx, HALO), inner],
            field.at[b, bottom, inner],
            halo_send.at[1, b],
            halo_recv.at[1, b],
            high,
        )

    def to_side(b):
        return remote(
            field.at[b, mid, y_rows],
            field.at[b, mid, y_land],
            halo_send.at[2, b],
            halo_recv.at[2, b],
            beside,
        )

    def once_low():
        part = pl.ds(0, HALO)
        return [
            remote(cour_ref.at[part], speed.at[top, inner], once_send.at[0], once_recv.at[0], low),
            remote(vel_ref.at[0, part], edge_x.at[top], once_send.at[1], once_recv.at[1], low),
        ]

    def once_high():
        part = pl.ds(cx - HALO, HALO)
        return [
            remote(cour_ref.at[part], speed.at[bottom, inner], once_send.at[2], once_recv.at[2], high),
            remote(vel_ref.at[0, part], edge_x.at[bottom], once_send.at[3], once_recv.at[3], high),
        ]

    def once_side():
        return [
            remote(
                cour_ref.at[:, y_own], speed.at[mid, y_land], once_send.at[4], once_recv.at[4], beside
            ),
            remote(
                vel_ref.at[1, :, y_own], edge_y.at[:, y_land], once_send.at[5], once_recv.at[5], beside
            ),
        ]

    lane = lax.broadcasted_iota(jnp.int32, (r_dev, r_dev), 1)
    row = lax.broadcasted_iota(jnp.int32, (r_dev, r_dev), 0)
    down = jnp.broadcast_to(owner_ref[...], (r_dev, r_dev)).astype(jnp.float32)
    across = jnp.sum(jnp.where(lane == row, down, 0.0), axis=0, keepdims=True)
    earlier = jnp.where((down == across) & (row < lane), 1.0, 0.0)
    rank = jnp.sum(earlier, axis=0, keepdims=True)
    spot = (across * float(cap) + rank).astype(jnp.int32)
    slot_id = lax.broadcasted_iota(jnp.int32, (slots, r_dev), 0)
    chosen = slot_id == spot
    code = (cell_ref[...] + 1).astype(jnp.float32)
    packed = jnp.sum(jnp.where(chosen, code, 0.0), axis=1, keepdims=True)
    codes_out[...] = jnp.broadcast_to(packed, codes_out.shape)

    field[0, HALO : HALO + cx, SIDE : SIDE + cy, :] = press_ref[...]
    speed[HALO : HALO + cx, SIDE : SIDE + cy, :] = cour_ref[...]
    edge_x[HALO : HALO + cx] = vel_ref[0]
    edge_y[:, SIDE : SIDE + cy, :] = vel_ref[1]
    now[...] = press_ref[...]
    records[...] = jnp.zeros_like(records)

    pl.semaphore_wait(barrier, subs - 1)

    @pl.when(has_low)
    def _():
        to_low(0).start()
        for copy in once_low():
            copy.start()

    @pl.when(has_high)
    def _():
        to_high(0).start()
        for copy in once_high():
            copy.start()

    to_side(0).start()
    for copy in once_side():
        copy.start()

    def swap(stage, source, landing, k):
        peer = peer_at(k)
        return remote(
            source.at[pl.ds(pl.multiple_of(peer * cap, 8), cap)],
            landing.at[pl.ds(pl.multiple_of(me * cap, 8), cap)],
            swap_send.at[stage, k],
            swap_recv.at[stage, k],
            place_of(peer),
        )

    def share(k):
        return remote(
            sums.at[me], sums.at[me], swap_send.at[2, k], swap_recv.at[2, k], place_of(peer_at(k))
        )

    def each(action):
        def one(k, carry):
            action(k)
            return carry

        lax.fori_loop(1, subs, one, 0)

    each(lambda k: swap(0, codes_out, codes_in, k).start())
    own = pl.ds(pl.multiple_of(me * cap, 8), cap)
    codes_in[own, :] = codes_out[own, :]

    shape = (cx, cy, cz)
    gx = lax.broadcasted_iota(jnp.int32, shape, 0) + ix * cx
    gy = lax.broadcasted_iota(jnp.int32, shape, 1) + iy * cy
    gz = lax.broadcasted_iota(jnp.int32, shape, 2)
    mark[...] = jnp.where((gx * (cy * count_y) + gy) * cz + gz == src_ref[0], 1.0, 0.0)

    @pl.when(has_low)
    def _():
        for copy in once_low():
            copy.wait_send()
        for copy in once_high():
            copy.wait_recv()

    @pl.when(has_high)
    def _():
        for copy in once_high():
            copy.wait_send()
        for copy in once_low():
            copy.wait_recv()

    for copy in once_side():
        copy.wait()

    fx = edge_x[1 : cx + 4]
    fy = edge_y[...]
    fz = vel_ref[2]
    spread = slope(fx[2 : 2 + cx], fx[1 : 1 + cx], fx[3 : 3 + cx], fx[0:cx])
    spread_y = slope(fy, shifted(fy, -1, 1), shifted(fy, 1, 1), shifted(fy, -2, 1))
    spread = spread + spread_y[:, SIDE : SIDE + cy]
    spread = spread + slope(fz, shifted_z(fz, -1), shifted_z(fz, 1), shifted_z(fz, -2))
    base[...] = cour_ref[...] * spread

    def grads(b, first, last):
        n = last - first
        fx = field[b, first : last + 2 * HALO, SIDE : SIDE + cy, :]
        m = n + 3
        grad_x = speed[first + 1 : last + 4, SIDE : SIDE + cy, :] * slope(
            fx[2 : 2 + m], fx[1 : 1 + m], fx[3 : 3 + m], fx[0:m]
        )
        fy = field[b, first + HALO : last + HALO]
        grad_y = speed[first + HALO : last + HALO] * slope(
            shifted(fy, 1, 1), fy, shifted(fy, 2, 1), shifted(fy, -1, 1)
        )
        fz = fy[:, SIDE : SIDE + cy]
        cour = cour_ref[first:last]
        grad_z = cour * slope(shifted_z(fz, 1), fz, shifted_z(fz, 2), shifted_z(fz, -1))
        return (grad_x, grad_y, grad_z, fz, cour)

    def update(b, first, last, amplitude):
        n = last - first
        grad_x, grad_y, grad_z, total, cour = grads(b, first, last)
        acc = slope(grad_x[2 : 2 + n], grad_x[1 : 1 + n], grad_x[3 : 3 + n], grad_x[0:n])
        acc_y = slope(
            grad_y, shifted(grad_y, -1, 1), shifted(grad_y, 1, 1), shifted(grad_y, -2, 1)
        )
        acc = acc + acc_y[:, SIDE : SIDE + cy]
        acc = acc + slope(
            grad_z, shifted_z(grad_z, -1), shifted_z(grad_z, 1), shifted_z(grad_z, -2)
        )
        fresh = now[first:last] + (cour * acc - base[first:last]) + amplitude * mark[first:last]
        now[first:last] = fresh
        field[1 - b, first + HALO : last + HALO, SIDE : SIDE + cy, :] = total + fresh

    def listen():
        each(lambda k: swap(0, codes_out, codes_in, k).wait())
        cell = codes_in[...].astype(jnp.int32) - 1
        bits = cz.bit_length() - 1
        cell_row = lax.shift_right_arithmetic(cell, jnp.full_like(cell, bits))
        cell_lane = cell & (cz - 1)
        lanes = lax.broadcasted_iota(jnp.int32, (slots, cz), 1)
        lane_hot[...] = jnp.where(cell_lane == lanes, 1.0, 0.0)
        for j in range(cx * cy // cz):
            rows_hot[:, j * cz : (j + 1) * cz] = jnp.where(
                cell_row == lanes + j * cz, 1.0, 0.0
            ).astype(jnp.bfloat16)

    def record(t):
        flat = now[...].reshape(cx * cy, cz)
        picked = jnp.zeros((slots, cz), jnp.float32)
        for part in pieces(flat, 3):
            picked = picked + jnp.dot(rows_hot[...], part, preferred_element_type=jnp.float32)
        value = jnp.sum(picked * lane_hot[...], axis=1, keepdims=True)
        lanes = lax.broadcasted_iota(jnp.int32, (slots, cz), 1)
        records[...] = jnp.where(lanes == t, value, records[...])

    def advance(t, carry):
        b = lax.rem(t, 2)
        more = t < steps - 1

        to_side(b).wait()
        amplitude = wave_ref[t]

        @pl.when(has_low)
        def _():
            to_low(b).wait_send()
            to_high(b).wait_recv()

        update(b, 0, HALO, amplitude)

        @pl.when(has_low & more)
        def _():
            to_low(1 - b).start()

        @pl.when(has_high)
        def _():
            to_high(b).wait_send()
            to_low(b).wait_recv()

        update(b, cx - HALO, cx, amplitude)

        @pl.when(has_high & more)
        def _():
            to_high(1 - b).start()

        update(b, HALO, cx - HALO, amplitude)

        @pl.when(more)
        def _():
            to_side(1 - b).start()

        @pl.when(t == 0)
        def _():
            listen()

        record(t)
        return carry

    lax.fori_loop(0, steps, advance, 0)

    each(lambda k: swap(1, records, returned, k).start())
    returned[own, :] = records[own, :]

    grad_x, grad_y, grad_z, _, _ = grads((steps - 1) % 2, 0, cx)
    vel_out[0] = vel_ref[0] - grad_x[2 : 2 + cx]
    vel_out[1] = vel_ref[1] - grad_y[:, SIDE : SIDE + cy]
    vel_out[2] = vel_ref[2] - grad_z
    press_out[...] = now[...]

    each(lambda k: swap(1, records, returned, k).wait())
    fetch.wait()
    height = table.shape[0]
    by_step = jnp.transpose(returned[...])[0:height]
    hot = jnp.where(chosen, 1.0, 0.0).astype(jnp.bfloat16)
    syn = jnp.zeros((height, r_dev), jnp.float32)
    for part in pieces(by_step, 3):
        syn = syn + jnp.dot(part, hot, preferred_element_type=jnp.float32)
    table[...] = jnp.zeros_like(table)
    table[:, 0:nt] = jnp.dot(
        syn, obs_ref[...], precision=lax.Precision.HIGHEST, preferred_element_type=jnp.float32
    )
    lines = table[...]
    step_id = lax.broadcasted_iota(jnp.int32, lines.shape, 0)
    for bit in range((steps - 1).bit_length()):
        lines = jnp.where((step_id & (1 << bit)) != 0, shifted(lines, 1 << bit, 1), lines)
    scale = 1.0 / math.sqrt(subs * r_dev * steps)
    sums[me] = jnp.sum(lines, axis=0, keepdims=True) * scale
    each(lambda k: share(k).start())
    each(lambda k: share(k).wait())
    xc_out[...] = jnp.sum(sums[...], axis=0)


def body(pressure, velocity, courant, observed, rec_owner, rec_cell, src_pos, wavelet):
    cx, cy, cz = pressure.shape
    count_x = lax.axis_size("sx")
    count_y = lax.axis_size("sy")
    subs = count_x * count_y
    r_dev, nt = observed.shape
    steps = wavelet.shape[0]
    nlag = nt - steps + 1
    cap = -(-max(2, 2 * r_dev // subs) // 8) * 8
    slots = subs * cap
    wide = -(-nt // 128) * 128
    height = -(-steps // 8) * 8
    deep = cx + 2 * HALO
    tall = cy + 2 * SIDE
    f32 = jnp.float32
    vmem = pl.BlockSpec(memory_space=pltpu.VMEM)
    smem = pl.BlockSpec(memory_space=pltpu.SMEM)
    press, vel, xc = pl.pallas_call(
        functools.partial(kernel, count_x, count_y, cap),
        out_shape=(
            jax.ShapeDtypeStruct((cx, cy, cz), f32),
            jax.ShapeDtypeStruct((3, cx, cy, cz), f32),
            jax.ShapeDtypeStruct((1, wide), f32),
        ),
        in_specs=[vmem] * 3 + [pl.BlockSpec(memory_space=pl.ANY)] + [vmem] * 2 + [smem] * 2,
        out_specs=(vmem,) * 3,
        scratch_shapes=[
            pltpu.VMEM((2, deep, tall, cz), f32),
            pltpu.VMEM((deep, tall, cz), f32),
            pltpu.VMEM((deep, cy, cz), f32),
            pltpu.VMEM((cx, tall, cz), f32),
            pltpu.VMEM((cx, cy, cz), f32),
            pltpu.VMEM((cx, cy, cz), f32),
            pltpu.VMEM((cx, cy, cz), f32),
            pltpu.VMEM((slots, cz), f32),
            pltpu.VMEM((slots, cz), f32),
            pltpu.VMEM((slots, cx * cy), jnp.bfloat16),
            pltpu.VMEM((slots, cz), f32),
            pltpu.VMEM((slots, cz), f32),
            pltpu.VMEM((slots, cz), f32),
            pltpu.VMEM((height, wide), f32),
            pltpu.VMEM((subs, 1, wide), f32),
            pltpu.SemaphoreType.DMA((3, 2)),
            pltpu.SemaphoreType.DMA((3, 2)),
            pltpu.SemaphoreType.DMA((6,)),
            pltpu.SemaphoreType.DMA((6,)),
            pltpu.SemaphoreType.DMA((3, subs)),
            pltpu.SemaphoreType.DMA((3, subs)),
            pltpu.VMEM((r_dev, nt), f32),
            pltpu.SemaphoreType.DMA((1,)),
        ],
        compiler_params=pltpu.CompilerParams(
            collective_id=0, has_side_effects=True, vmem_limit_bytes=40 * 2**20
        ),
    )(
        pressure,
        velocity,
        courant,
        observed,
        rec_owner,
        rec_cell.reshape(1, r_dev),
        src_pos,
        wavelet,
    )
    return (press, vel, xc[0, :nlag])


def solution(mesh):
    placed = (
        P(("shot", "sx"), "sy", None),
        P(None, ("shot", "sx"), "sy", None),
        P("sx", "sy", None),
        P(("shot", "sx", "sy"), None),
        P(("shot", "sx", "sy"), None),
        P(("shot", "sx", "sy")),
        P("shot"),
        P(),
    )
    return jax.shard_map(
        body,
        mesh=mesh,
        in_specs=placed,
        out_specs=(P(("shot", "sx"), "sy", None), P(None, ("shot", "sx"), "sy", None), P("shot")),
        check_vma=False,
    )
```

```python
import functools
import math

import jax
import jax.numpy as jnp
from jax import lax
from jax.experimental import pallas as pl
from jax.experimental.pallas import tpu as pltpu
from jax.sharding import PartitionSpec as P

c_one = 9.0 / 8.0
c_two = -1.0 / 24.0
HALO = 3
SIDE = 8


def pieces(value, count):
    parts = []
    for _ in range(count):
        part = value.astype(jnp.bfloat16)
        parts.append(part)
        value = value - part.astype(jnp.float32)
    return parts


def slope(a, b, c, d):
    return c_one * (a - b) + c_two * (c - d)


def shifted(f, k, axis):
    count = f.shape[axis]
    return pltpu.roll(f, (-k) % count, axis)


def shifted_z(f, k):
    count = f.shape[-1]
    place = lax.broadcasted_iota(jnp.int32, f.shape, f.ndim - 1)
    keep = place < count - k if k > 0 else place >= -k
    return jnp.where(keep, shifted(f, k, f.ndim - 1), 0.0)


def kernel(
    count_x,
    count_y,
    cap,
    press_ref,
    vel_ref,
    cour_ref,
    obs_far,
    owner_ref,
    cell_ref,
    src_ref,
    wave_ref,
    press_out,
    vel_out,
    xc_out,
    field,
    speed,
    edge_x,
    edge_y,
    base,
    mark,
    now,
    codes_out,
    codes_in,
    rows_hot,
    lane_hot,
    records,
    returned,
    table,
    sums,
    halo_send,
    halo_recv,
    once_send,
    once_recv,
    swap_send,
    swap_recv,
    obs_ref,
    obs_sem,
):
    cx, cy, cz = press_ref.shape
    r_dev, nt = obs_ref.shape
    steps = wave_ref.shape[0]
    nlag = nt - steps + 1
    subs = count_x * count_y
    slots = subs * cap
    ix = lax.axis_index("sx")
    iy = lax.axis_index("sy")
    me = ix * count_y + iy
    inner = pl.ds(SIDE, cy)

    def place_of(peer):
        return {"sx": peer // count_y, "sy": peer % count_y}

    def peer_at(k):
        return lax.rem(me + k, subs)

    fetch = pltpu.make_async_copy(obs_far, obs_ref, obs_sem.at[0])
    fetch.start()
    field[...] = jnp.zeros_like(field)
    speed[...] = jnp.zeros_like(speed)
    edge_x[...] = jnp.zeros_like(edge_x)
    edge_y[...] = jnp.zeros_like(edge_y)

    barrier = pltpu.get_barrier_semaphore()

    def greet(k, carry):
        pl.semaphore_signal(
            barrier, inc=1, device_id=place_of(peer_at(k)), device_id_type=pl.DeviceIdType.MESH
        )
        return carry

    lax.fori_loop(1, subs, greet, 0)

    low = {"sx": ix - 1}
    high = {"sx": ix + 1}
    beside = {"sy": 1 - iy}
    has_low = ix > 0
    has_high = ix < count_x - 1

    def remote(src, dst, send, recv, device):
        return pltpu.make_async_remote_copy(
            src_ref=src,
            dst_ref=dst,
            send_sem=send,
            recv_sem=recv,
            device_id=device,
            device_id_type=pl.DeviceIdType.MESH,
        )

    y_from = pl.multiple_of(SIDE * (1 - iy), SIDE)
    y_to = pl.multiple_of((SIDE + cy) * iy, SIDE)
    y_rows = pl.ds(y_from + SIDE, SIDE)
    y_land = pl.ds(y_to, SIDE)
    y_own = pl.ds(y_from, SIDE)
    mid = pl.ds(HALO, cx)
    top = pl.ds(HALO + cx, HALO)
    bottom = pl.ds(0, HALO)

    def to_low(b):
        return remote(
            field.at[b, pl.ds(HALO, HALO), inner],
            field.at[b, top, inner],
            halo_send.at[0, b],
            halo_recv.at[0, b],
            low,
        )

    def to_high(b):
        return remote(
            field.at[b, pl.ds(cx, HALO), inner],
            field.at[b, bottom, inner],
            halo_send.at[1, b],
            halo_recv.at[1, b],
            high,
        )

    def to_side(b):
        return remote(
            field.at[b, mid, y_rows],
            field.at[b, mid, y_land],
            halo_send.at[2, b],
            halo_recv.at[2, b],
            beside,
        )

    def once_low():
        part = pl.ds(0, HALO)
        return [
            remote(cour_ref.at[part], speed.at[top, inner], once_send.at[0], once_recv.at[0], low),
            remote(vel_ref.at[0, part], edge_x.at[top], once_send.at[1], once_recv.at[1], low),
        ]

    def once_high():
        part = pl.ds(cx - HALO, HALO)
        return [
            remote(cour_ref.at[part], speed.at[bottom, inner], once_send.at[2], once_recv.at[2], high),
            remote(vel_ref.at[0, part], edge_x.at[bottom], once_send.at[3], once_recv.at[3], high),
        ]

    def once_side():
        return [
            remote(
                cour_ref.at[:, y_own], speed.at[mid, y_land], once_send.at[4], once_recv.at[4], beside
            ),
            remote(
                vel_ref.at[1, :, y_own], edge_y.at[:, y_land], once_send.at[5], once_recv.at[5], beside
            ),
        ]

    lane = lax.broadcasted_iota(jnp.int32, (r_dev, r_dev), 1)
    row = lax.broadcasted_iota(jnp.int32, (r_dev, r_dev), 0)
    down = jnp.broadcast_to(owner_ref[...], (r_dev, r_dev)).astype(jnp.float32)
    across = jnp.sum(jnp.where(lane == row, down, 0.0), axis=0, keepdims=True)
    earlier = jnp.where((down == across) & (row < lane), 1.0, 0.0)
    rank = jnp.sum(earlier, axis=0, keepdims=True)
    spot = (across * float(cap) + rank).astype(jnp.int32)
    slot_id = lax.broadcasted_iota(jnp.int32, (slots, r_dev), 0)
    chosen = slot_id == spot
    code = (cell_ref[...] + 1).astype(jnp.float32)
    packed = jnp.sum(jnp.where(chosen, code, 0.0), axis=1, keepdims=True)
    codes_out[...] = jnp.broadcast_to(packed, codes_out.shape)

    field[0, HALO : HALO + cx, SIDE : SIDE + cy, :] = press_ref[...]
    speed[HALO : HALO + cx, SIDE : SIDE + cy, :] = cour_ref[...]
    edge_x[HALO : HALO + cx] = vel_ref[0]
    edge_y[:, SIDE : SIDE + cy, :] = vel_ref[1]
    now[...] = press_ref[...]
    records[...] = jnp.zeros_like(records)

    pl.semaphore_wait(barrier, subs - 1)

    @pl.when(has_low)
    def _():
        to_low(0).start()
        for copy in once_low():
            copy.start()

    @pl.when(has_high)
    def _():
        to_high(0).start()
        for copy in once_high():
            copy.start()

    to_side(0).start()
    for copy in once_side():
        copy.start()

    def swap(stage, source, landing, k):
        peer = peer_at(k)
        return remote(
            source.at[pl.ds(pl.multiple_of(peer * cap, 8), cap)],
            landing.at[pl.ds(pl.multiple_of(me * cap, 8), cap)],
            swap_send.at[stage, k],
            swap_recv.at[stage, k],
            place_of(peer),
        )

    def share(k):
        return remote(
            sums.at[me], sums.at[me], swap_send.at[2, k], swap_recv.at[2, k], place_of(peer_at(k))
        )

    def each(action):
        def one(k, carry):
            action(k)
            return carry

        lax.fori_loop(1, subs, one, 0)

    each(lambda k: swap(0, codes_out, codes_in, k).start())
    own = pl.ds(pl.multiple_of(me * cap, 8), cap)
    codes_in[own, :] = codes_out[own, :]

    shape = (cx, cy, cz)
    gx = lax.broadcasted_iota(jnp.int32, shape, 0) + ix * cx
    gy = lax.broadcasted_iota(jnp.int32, shape, 1) + iy * cy
    gz = lax.broadcasted_iota(jnp.int32, shape, 2)
    mark[...] = jnp.where((gx * (cy * count_y) + gy) * cz + gz == src_ref[0], 1.0, 0.0)

    @pl.when(has_low)
    def _():
        for copy in once_low():
            copy.wait_send()
        for copy in once_high():
            copy.wait_recv()

    @pl.when(has_high)
    def _():
        for copy in once_high():
            copy.wait_send()
        for copy in once_low():
            copy.wait_recv()

    for copy in once_side():
        copy.wait()

    fx = edge_x[1 : cx + 4]
    fy = edge_y[...]
    fz = vel_ref[2]
    spread = slope(fx[2 : 2 + cx], fx[1 : 1 + cx], fx[3 : 3 + cx], fx[0:cx])
    spread_y = slope(fy, shifted(fy, -1, 1), shifted(fy, 1, 1), shifted(fy, -2, 1))
    spread = spread + spread_y[:, SIDE : SIDE + cy]
    spread = spread + slope(fz, shifted_z(fz, -1), shifted_z(fz, 1), shifted_z(fz, -2))
    base[...] = cour_ref[...] * spread

    def grads(b, first, last):
        n = last - first
        fx = field[b, first : last + 2 * HALO, SIDE : SIDE + cy, :]
        m = n + 3
        grad_x = speed[first + 1 : last + 4, SIDE : SIDE + cy, :] * slope(
            fx[2 : 2 + m], fx[1 : 1 + m], fx[3 : 3 + m], fx[0:m]
        )
        fy = field[b, first + HALO : last + HALO]
        grad_y = speed[first + HALO : last + HALO] * slope(
            shifted(fy, 1, 1), fy, shifted(fy, 2, 1), shifted(fy, -1, 1)
        )
        fz = fy[:, SIDE : SIDE + cy]
        cour = cour_ref[first:last]
        grad_z = cour * slope(shifted_z(fz, 1), fz, shifted_z(fz, 2), shifted_z(fz, -1))
        return (grad_x, grad_y, grad_z, fz, cour)

    def early(b, first, last, amplitude):
        fy = field[b, first + HALO : last + HALO]
        grad_y = speed[first + HALO : last + HALO] * slope(
            shifted(fy, 1, 1), fy, shifted(fy, 2, 1), shifted(fy, -1, 1)
        )
        fz = fy[:, SIDE : SIDE + cy]
        cour = cour_ref[first:last]
        grad_z = cour * slope(shifted_z(fz, 1), fz, shifted_z(fz, 2), shifted_z(fz, -1))
        acc_y = slope(
            grad_y, shifted(grad_y, -1, 1), shifted(grad_y, 1, 1), shifted(grad_y, -2, 1)
        )
        acc = acc_y[:, SIDE : SIDE + cy] + slope(
            grad_z, shifted_z(grad_z, -1), shifted_z(grad_z, 1), shifted_z(grad_z, -2)
        )
        now[first:last] = now[first:last] + (
            (cour * acc - base[first:last]) + amplitude * mark[first:last]
        )

    def late(b, first, last):
        n = last - first
        m = n + 3
        fx = field[b, first : last + 2 * HALO, SIDE : SIDE + cy, :]
        grad_x = speed[first + 1 : last + 4, SIDE : SIDE + cy, :] * slope(
            fx[2 : 2 + m], fx[1 : 1 + m], fx[3 : 3 + m], fx[0:m]
        )
        acc = slope(grad_x[2 : 2 + n], grad_x[1 : 1 + n], grad_x[3 : 3 + n], grad_x[0:n])
        fresh = now[first:last] + cour_ref[first:last] * acc
        now[first:last] = fresh
        field[1 - b, first + HALO : last + HALO, SIDE : SIDE + cy, :] = (
            fx[HALO : HALO + n] + fresh
        )

    def listen():
        each(lambda k: swap(0, codes_out, codes_in, k).wait())
        cell = codes_in[...].astype(jnp.int32) - 1
        bits = cz.bit_length() - 1
        cell_row = lax.shift_right_arithmetic(cell, jnp.full_like(cell, bits))
        cell_lane = cell & (cz - 1)
        lanes = lax.broadcasted_iota(jnp.int32, (slots, cz), 1)
        lane_hot[...] = jnp.where(cell_lane == lanes, 1.0, 0.0)
        for j in range(cx * cy // cz):
            rows_hot[:, j * cz : (j + 1) * cz] = jnp.where(
                cell_row == lanes + j * cz, 1.0, 0.0
            ).astype(jnp.bfloat16)

    def record(t):
        flat = now[...].reshape(cx * cy, cz)
        picked = jnp.zeros((slots, cz), jnp.float32)
        for part in pieces(flat, 3):
            picked = picked + jnp.dot(rows_hot[...], part, preferred_element_type=jnp.float32)
        value = jnp.sum(picked * lane_hot[...], axis=1, keepdims=True)
        lanes = lax.broadcasted_iota(jnp.int32, (slots, cz), 1)
        records[...] = jnp.where(lanes == t, value, records[...])

    def advance(t, carry):
        b = lax.rem(t, 2)
        more = t < steps - 1

        to_side(b).wait()
        amplitude = wave_ref[t]
        early(b, 0, HALO, amplitude)
        early(b, cx - HALO, cx, amplitude)

        @pl.when(has_low)
        def _():
            to_low(b).wait_send()
            to_high(b).wait_recv()

        late(b, 0, HALO)

        @pl.when(has_low & more)
        def _():
            to_low(1 - b).start()

        @pl.when(has_high)
        def _():
            to_high(b).wait_send()
            to_low(b).wait_recv()

        late(b, cx - HALO, cx)

        @pl.when(has_high & more)
        def _():
            to_high(1 - b).start()

        early(b, HALO, cx - HALO, amplitude)
        late(b, HALO, cx - HALO)

        @pl.when(more)
        def _():
            to_side(1 - b).start()

        @pl.when(t == 0)
        def _():
            listen()

        record(t)
        return carry

    lax.fori_loop(0, steps, advance, 0)

    each(lambda k: swap(1, records, returned, k).start())
    returned[own, :] = records[own, :]

    grad_x, grad_y, grad_z, _, _ = grads((steps - 1) % 2, 0, cx)
    vel_out[0] = vel_ref[0] - grad_x[2 : 2 + cx]
    vel_out[1] = vel_ref[1] - grad_y[:, SIDE : SIDE + cy]
    vel_out[2] = vel_ref[2] - grad_z
    press_out[...] = now[...]

    each(lambda k: swap(1, records, returned, k).wait())
    fetch.wait()
    height = table.shape[0]
    by_step = jnp.transpose(returned[...])[0:height]
    hot = jnp.where(chosen, 1.0, 0.0).astype(jnp.bfloat16)
    syn = jnp.zeros((height, r_dev), jnp.float32)
    for part in pieces(by_step, 3):
        syn = syn + jnp.dot(part, hot, preferred_element_type=jnp.float32)
    table[...] = jnp.zeros_like(table)
    table[:, 0:nt] = jnp.dot(
        syn, obs_ref[...], precision=lax.Precision.HIGHEST, preferred_element_type=jnp.float32
    )
    lines = table[...]
    step_id = lax.broadcasted_iota(jnp.int32, lines.shape, 0)
    for bit in range((steps - 1).bit_length()):
        lines = jnp.where((step_id & (1 << bit)) != 0, shifted(lines, 1 << bit, 1), lines)
    scale = 1.0 / math.sqrt(subs * r_dev * steps)
    sums[me] = jnp.sum(lines, axis=0, keepdims=True) * scale
    each(lambda k: share(k).start())
    each(lambda k: share(k).wait())
    xc_out[...] = jnp.sum(sums[...], axis=0)


def body(pressure, velocity, courant, observed, rec_owner, rec_cell, src_pos, wavelet):
    cx, cy, cz = pressure.shape
    count_x = lax.axis_size("sx")
    count_y = lax.axis_size("sy")
    subs = count_x * count_y
    r_dev, nt = observed.shape
    steps = wavelet.shape[0]
    nlag = nt - steps + 1
    cap = -(-max(2, 2 * r_dev // subs) // 8) * 8
    slots = subs * cap
    wide = -(-nt // 128) * 128
    height = -(-steps // 8) * 8
    deep = cx + 2 * HALO
    tall = cy + 2 * SIDE
    f32 = jnp.float32
    vmem = pl.BlockSpec(memory_space=pltpu.VMEM)
    smem = pl.BlockSpec(memory_space=pltpu.SMEM)
    press, vel, xc = pl.pallas_call(
        functools.partial(kernel, count_x, count_y, cap),
        out_shape=(
            jax.ShapeDtypeStruct((cx, cy, cz), f32),
            jax.ShapeDtypeStruct((3, cx, cy, cz), f32),
            jax.ShapeDtypeStruct((1, wide), f32),
        ),
        in_specs=[vmem] * 3 + [pl.BlockSpec(memory_space=pl.ANY)] + [vmem] * 2 + [smem] * 2,
        out_specs=(vmem,) * 3,
        scratch_shapes=[
            pltpu.VMEM((2, deep, tall, cz), f32),
            pltpu.VMEM((deep, tall, cz), f32),
            pltpu.VMEM((deep, cy, cz), f32),
            pltpu.VMEM((cx, tall, cz), f32),
            pltpu.VMEM((cx, cy, cz), f32),
            pltpu.VMEM((cx, cy, cz), f32),
            pltpu.VMEM((cx, cy, cz), f32),
            pltpu.VMEM((slots, cz), f32),
            pltpu.VMEM((slots, cz), f32),
            pltpu.VMEM((slots, cx * cy), jnp.bfloat16),
            pltpu.VMEM((slots, cz), f32),
            pltpu.VMEM((slots, cz), f32),
            pltpu.VMEM((slots, cz), f32),
            pltpu.VMEM((height, wide), f32),
            pltpu.VMEM((subs, 1, wide), f32),
            pltpu.SemaphoreType.DMA((3, 2)),
            pltpu.SemaphoreType.DMA((3, 2)),
            pltpu.SemaphoreType.DMA((6,)),
            pltpu.SemaphoreType.DMA((6,)),
            pltpu.SemaphoreType.DMA((3, subs)),
            pltpu.SemaphoreType.DMA((3, subs)),
            pltpu.VMEM((r_dev, nt), f32),
            pltpu.SemaphoreType.DMA((1,)),
        ],
        compiler_params=pltpu.CompilerParams(
            collective_id=0, has_side_effects=True, vmem_limit_bytes=40 * 2**20
        ),
    )(
        pressure,
        velocity,
        courant,
        observed,
        rec_owner,
        rec_cell.reshape(1, r_dev),
        src_pos,
        wavelet,
    )
    return (press, vel, xc[0, :nlag])


def solution(mesh):
    placed = (
        P(("shot", "sx"), "sy", None),
        P(None, ("shot", "sx"), "sy", None),
        P("sx", "sy", None),
        P(("shot", "sx", "sy"), None),
        P(("shot", "sx", "sy"), None),
        P(("shot", "sx", "sy")),
        P("shot"),
        P(),
    )
    return jax.shard_map(
        body,
        mesh=mesh,
        in_specs=placed,
        out_specs=(P(("shot", "sx"), "sy", None), P(None, ("shot", "sx"), "sy", None), P("shot")),
        check_vma=False,
    )
```
